256 devices in a mesh: row: 16 (over y_lo, z), col: 16 (over x, y_hi, core).
Axes of the slice: x: 4, y: 4 (y_hi: 2, y_lo: 2; y = y_hi * 2 + y_lo), z: 8, core: 2. Of those that a mesh axis runs over, the one named last changes fastest.
Arguments:
- momentum: float32 [4096, 7168], P('row', 'col'), may hold values from -2.2 to 2.2
Outputs:
- update: float32 [4096, 7168], P('row', 'col')
The draws below stay inside these ranges and needn't reach their ends.
All inputs are finite; a program needn't handle non-finite values.
Results may differ from the reference program's by a relative error of at most 0.000082.
Values sent between devices are 32-bit elements; how exact they have to be, the bound alone decides.
No kernel may reach another device: no remote copies, remote signals or barrier semaphores. Data moves between devices by JAX's collectives and lax.ppermute only.
A program may use at most 64 MiB of HBM per device.

```python
import jax
import jax.numpy as jnp
from jax import lax

ROWS = 4096
COLS = 7168


def draw_momentum(key, part):
    key = jax.random.fold_in(key, 7)
    values = 0.55 * jax.random.truncated_normal(key, -4.0, 4.0, (ROWS, COLS), jnp.float32)
    return values


def setup_inputs(seed: int = 0) -> dict:
    streams_of = jax.random.split(jax.random.key(seed), 2)
    return {
        "momentum": draw_momentum(jax.random.fold_in(streams_of[1], 71), 0),
    }


weight_lin = 3.4445
weight_cub = -4.7750
weight_quint = 2.0315


def reference(momentum):
    highest = lax.Precision.HIGHEST
    gram = jnp.dot(momentum, momentum.T, precision=highest, preferred_element_type=jnp.float32) / COLS
    square = jnp.dot(gram, gram, precision=highest, preferred_element_type=jnp.float32)
    poly = weight_cub * gram + weight_quint * square
    return weight_lin * momentum + jnp.dot(poly, momentum, precision=highest, preferred_element_type=jnp.float32)
```

```python
import jax
import jax.numpy as jnp
from jax import lax
from jax.sharding import Mesh
from jax.sharding import PartitionSpec as P

COLS = 7168
BLOCK = 256

weight_lin = 3.4445
weight_cub = -4.775
weight_quint = 2.0315

Y_LO, Z, X, Y_HI, CORE = "y_lo", "z", "x", "y_hi", "core"
SIZES = (2, 8, 4, 2, 2)


def dot(left, right, left_dim, right_dim):
    return lax.dot_general(
        left,
        right,
        (((left_dim,), (right_dim,)), ((), ())),
        precision=lax.Precision.HIGH,
        preferred_element_type=jnp.float32,
    )


def z_shift(value, step):
    return lax.ppermute(value, Z, [(i, (i + step) % 8) for i in range(8)])


def y_swap(value):
    return lax.ppermute(value, Y_LO, [(0, 1), (1, 0)])


def core_swap(value):
    return lax.ppermute(value, CORE, [(0, 1), (1, 0)])


def plane_shift(value, dx, dy):
    perm = []
    for x in range(4):
        for y in range(2):
            perm.append((x * 2 + y, ((x + dx) % 4) * 2 + (y + dy) % 2))
    return lax.ppermute(value, (X, Y_HI), perm)


def halves(value):
    middle = value.shape[0] // 2
    return [value[:middle], value[middle:]]


def gather(own):
    parts = []
    for part in halves(own):
        p1 = z_shift(part, -1)
        m1 = z_shift(part, 1)
        p2 = z_shift(p1, -1)
        m2 = z_shift(m1, 1)
        s = y_swap(p2)
        parts.append((m2, m1, part, p1, p2, s))
    return [jnp.concatenate(pair, axis=0) for pair in zip(*parts)]


def reduce(m2, m1, o, p1, p2, s):
    out = []
    for a, b, c, d, e, f in zip(*map(halves, (m2, m1, o, p1, p2, s))):
        plus = z_shift(d + z_shift(e + y_swap(f), 1), 1)
        minus = z_shift(b + z_shift(a, -1), -1)
        out.append(c + plus + minus)
    return jnp.concatenate(out, axis=0)


def rotate(items, index):
    n = len(items)
    shift = 1
    while shift < n:
        bit = (index // shift) % 2 == 1
        items = [jnp.where(bit, items[(k - shift) % n], items[k]) for k in range(n)]
        shift *= 2
    return items


def sum_columns(value):
    x, y, core = lax.axis_index(X), lax.axis_index(Y_HI), lax.axis_index(CORE)
    top, bottom = value[:128], value[128:]
    keep = jnp.where(core == 0, top, bottom) + core_swap(jnp.where(core == 0, bottom, top))
    keep = keep.reshape(8, 16, -1)
    total = None
    for dx in (2, 1, 3, 0):
        for dy in (1, 0):
            place = ((x + dx) % 4) * 2 + (y + dy) % 2
            chunk = lax.dynamic_index_in_dim(keep, place, 0, keepdims=False)
            if dx or dy:
                chunk = plane_shift(chunk, dx, dy)
            total = chunk if total is None else total + chunk
    return total


def spread_columns(chunk):
    x, y, core = lax.axis_index(X), lax.axis_index(Y_HI), lax.axis_index(CORE)
    rows = []
    for dx in range(4):
        pair = [plane_shift(chunk, dx, dy) if dx or dy else chunk for dy in (0, 1)]
        rows.append(jnp.concatenate(rotate(pair, y), axis=0))
    ordered = rotate([rows[0], rows[3], rows[2], rows[1]], x)
    mine = jnp.concatenate(ordered, axis=0)
    other = core_swap(mine)
    return jnp.concatenate(rotate([mine, other], core), axis=0)


def apply(gram, blocks):
    m2, m1, o, p1, p2, s = blocks
    g_s, g_o, g_m2, g_m1 = gram
    y_s = dot(jnp.concatenate([m2, m1, o, p1, p2], axis=1), g_s, 1, 1)
    from_s = dot(s, g_s[:, 256:1024], 1, 0)
    from_o = dot(o, g_o[:, 256:], 1, 0)
    y_o = dot(jnp.concatenate([o, p1, p2], axis=1), g_o, 1, 1)
    y_m1 = dot(p2, g_m1, 1, 1)
    y_m2 = dot(p2, g_m2, 1, 1)
    y_p2 = dot(m1, g_m1, 1, 0)
    return (
        y_m2,
        y_m1 + from_s[:, :256],
        y_o + from_s[:, 256:512],
        from_o[:, :256] + from_s[:, 512:],
        from_o[:, 256:] + y_p2,
        y_s,
    )


def shards(momentum):
    own = momentum.T
    blocks = gather(own)
    m2, m1, o, p1, p2, s = blocks
    partial_value = jnp.concatenate(
        [
            dot(s, jnp.concatenate([m2, m1, o, p1, p2], axis=1), 0, 0),
            dot(o, jnp.concatenate([o, p1, p2], axis=1), 0, 0),
            dot(m2, p2, 0, 0),
            dot(m1, p2, 0, 0),
        ],
        axis=1,
    )
    gram = spread_columns(sum_columns(partial_value) / COLS)
    gram = (gram[:, :1280], gram[:, 1280:2048], gram[:, 2048:2304], gram[:, 2304:])
    first = reduce(*apply(gram, blocks))
    inner = weight_cub * own + weight_quint * first
    second = reduce(*apply(gram, gather(inner)))
    return (weight_lin * own + second).T


def solution(mesh):
    parts = Mesh(mesh.devices.reshape(SIZES), (Y_LO, Z, X, Y_HI, CORE))
    spec = P((Y_LO, Z), (X, Y_HI, CORE))
    return jax.shard_map(shards, mesh=parts, in_specs=(spec,), out_specs=spec, check_vma=False)
```

```python
import jax
import jax.numpy as jnp
from jax import lax
from jax.sharding import Mesh
from jax.sharding import PartitionSpec as P

COLS = 7168

weight_lin = 3.4445
weight_cub = -4.775
weight_quint = 2.0315

Y_LO, Z, X, Y_HI, CORE = "y_lo", "z", "x", "y_hi", "core"
SIZES = (2, 8, 4, 2, 2)


def dot(left, right, left_dim, right_dim):
    return lax.dot_general(
        left,
        right,
        (((left_dim,), (right_dim,)), ((), ())),
        precision=lax.Precision.HIGH,
        preferred_element_type=jnp.float32,
    )


def z_shift(value, step):
    return lax.ppermute(value, Z, [(i, (i + step) % 8) for i in range(8)])


def y_swap(value):
    return lax.ppermute(value, Y_LO, [(0, 1), (1, 0)])


def core_swap(value):
    return lax.ppermute(value, CORE, [(0, 1), (1, 0)])


def plane_shift(value, dx, dy):
    perm = []
    for x in range(4):
        for y in range(2):
            perm.append((x * 2 + y, ((x + dx) % 4) * 2 + (y + dy) % 2))
    return lax.ppermute(value, (X, Y_HI), perm)


def swap_rows(value):
    middle = value.shape[0] // 2
    return jnp.concatenate([value[middle:], value[:middle]], axis=0)


def swap_lanes(value):
    return jnp.concatenate([value[:, 128:], value[:, :128]], axis=1)


def z_line(own):
    middle = own.shape[0] // 2
    p1, m1 = z_shift(own, -1), z_shift(own, 1)
    p2, m2 = z_shift(p1, -1), z_shift(m1, 1)
    p3, m3 = z_shift(p2, -1), z_shift(m2, 1)
    far = jnp.concatenate([z_shift(p3[:middle], -1), z_shift(m3[middle:], 1)], axis=0)
    return [own, p1, p2, p3, far, m3, m2, m1]


NEAR, FAR = (0, 1, 7, 2, 6), (3, 5, 4)


def sum_plane(value):
    x, y = lax.axis_index(X), lax.axis_index(Y_HI)
    value = value.reshape(-1, 8, 16, 512)
    total = None
    for dx in (2, 1, 3, 0):
        for dy in (1, 0):
            place = ((x + dx) % 4) * 2 + (y + dy) % 2
            chunk = lax.dynamic_index_in_dim(value, place, 1, keepdims=False)
            if dx or dy:
                chunk = plane_shift(chunk, dx, dy)
            total = chunk if total is None else total + chunk
    return total


def products(line, pair):
    mine, others = [None] * 8, [None] * 8
    for group in (NEAR, FAR):
        value = dot(jnp.concatenate([line[i] for i in group], axis=1), pair, 0, 0)
        value = sum_plane(value.reshape(len(group), 128, 512))
        crossed = y_swap(value[:, :, 256:])
        for place, i in enumerate(group):
            mine[i] = value[place, :, :256]
            others[i] = crossed[place]
    return jnp.stack([jnp.stack(mine), jnp.stack(others)])


def rotate(items, index):
    n = len(items)
    shift = 1
    while shift < n:
        bit = (index // shift) % 2 == 1
        items = [jnp.where(bit, items[(k - shift) % n], items[k]) for k in range(n)]
        shift *= 2
    return items


def spread_plane(chunk):
    x, y = lax.axis_index(X), lax.axis_index(Y_HI)
    rows = []
    for dx in range(4):
        pair = [plane_shift(chunk, dx, dy) if dx or dy else chunk for dy in (0, 1)]
        rows.append(jnp.stack(rotate(pair, y), axis=1))
    ordered = rotate([rows[0], rows[3], rows[2], rows[1]], x)
    return jnp.stack(ordered, axis=1).reshape(16, 128, -1)


def shards(momentum):
    core = lax.axis_index(CORE)
    own = momentum.T
    low, high = own[:, :128], own[:, 128:]
    half = jnp.concatenate([jnp.where(core == 0, low, high), core_swap(jnp.where(core == 0, high, low))], axis=0)
    row = jnp.concatenate([half, swap_rows(core_swap(half))], axis=1)
    partner = y_swap(half)
    partner_row = jnp.concatenate([partner, swap_rows(core_swap(partner))], axis=1)
    line = z_line(half)
    gram = products(line, jnp.concatenate([row, partner_row], axis=1)) / COLS

    flat = gram.reshape(256, 256)
    gram_row = jnp.concatenate([flat, swap_lanes(core_swap(flat))], axis=0)
    gram_half = gram_row[:, :128]
    crossed = y_swap(gram_half).reshape(2, 2, 128, 128)[:, ::-1].reshape(512, 128)
    gram_partner = jnp.concatenate([crossed, swap_rows(core_swap(crossed))], axis=1)
    gram_line = z_line(gram_half)
    turned = [jnp.roll(gram_line[i].reshape(4, 8, 16, 128), i, axis=1).reshape(512, 128) for i in range(8)]
    square = products(turned, jnp.concatenate([gram_row, gram_partner], axis=1))

    poly = weight_cub * gram + weight_quint * square
    whole = spread_plane(poly.reshape(16, 16, 256)).reshape(2048, 256)
    partner, _ = lax.optimization_barrier((partner, gram_line[4]))
    both = jnp.concatenate(line + z_line(partner), axis=1)
    product = dot(both, whole, 1, 0)
    product = product[:448] + swap_lanes(core_swap(product[448:]))
    product = jnp.where(core == 0, product, swap_lanes(product))
    return (weight_lin * own + product).T


def solution(mesh):
    parts = Mesh(mesh.devices.reshape(SIZES), (Y_LO, Z, X, Y_HI, CORE))
    spec = P((Y_LO, Z), (X, Y_HI, CORE))
    return jax.shard_map(shards, mesh=parts, in_specs=(spec,), out_specs=spec, check_vma=False)
```

```python
import jax
import jax.numpy as jnp
from jax import lax
from jax.sharding import Mesh
from jax.sharding import PartitionSpec as P

COLS = 7168

weight_lin = 3.4445
weight_cub = -4.775
weight_quint = 2.0315

Y_LO, Z, X, Y_HI, CORE = "y_lo", "z", "x", "y_hi", "core"
SIZES = (2, 8, 4, 2, 2)


def dot(left, right, left_dim, right_dim):
    return lax.dot_general(
        left,
        right,
        (((left_dim,), (right_dim,)), ((), ())),
        precision=lax.Precision.HIGH,
        preferred_element_type=jnp.float32,
    )


def z_shift(value, step):
    return lax.ppermute(value, Z, [(i, (i + step) % 8) for i in range(8)])


def y_swap(value):
    return lax.ppermute(value, Y_LO, [(0, 1), (1, 0)])


def core_swap(value):
    return lax.ppermute(value, CORE, [(0, 1), (1, 0)])


def y_hi_swap(value):
    return lax.ppermute(value, Y_HI, [(0, 1), (1, 0)])


def x_shift(value, step):
    return lax.ppermute(value, X, [(i, (i + step) % 4) for i in range(4)])


def after(value, *others):
    return lax.optimization_barrier((value, *others))[0]


def z_line(own):
    middle = own.shape[0] // 2
    p1, m1 = z_shift(own, -1), z_shift(own, 1)
    p2, m2 = z_shift(p1, -1), z_shift(m1, 1)
    p3, m3 = z_shift(p2, -1), z_shift(m2, 1)
    far = jnp.concatenate([z_shift(p3[:middle], -1), z_shift(m3[middle:], 1)], axis=0)
    return own, p1, m1, p2, m2, p3, m3, far


def sum_x(value):
    x = lax.axis_index(X)
    total = None
    for step in (2, 1, 3, 0):
        chunk = lax.dynamic_index_in_dim(value, (x + step) % 4, 1, keepdims=False)
        if step:
            chunk = x_shift(chunk, step)
        total = chunk if total is None else total + chunk
    return total


def sum_y_hi(value):
    low, high = value[..., 0, :, :], value[..., 1, :, :]
    first = lax.axis_index(Y_HI) == 0
    return jnp.where(first, low, high) + y_hi_swap(jnp.where(first, high, low))


def spread_y_hi(value):
    other = y_hi_swap(value)
    first = lax.axis_index(Y_HI) == 0
    return jnp.stack([jnp.where(first, value, other), jnp.where(first, other, value)], axis=-3)


def rotate(items, index):
    n = len(items)
    shift = 1
    while shift < n:
        bit = (index // shift) % 2 == 1
        items = [jnp.where(bit, items[(k - shift) % n], items[k]) for k in range(n)]
        shift *= 2
    return items


def spread_x(value):
    items = [value, x_shift(value, 3), x_shift(value, 2), x_shift(value, 1)]
    return jnp.stack(rotate(items, lax.axis_index(X)), axis=1)


def share(lines, gram):
    value, start = None, 0
    for line in lines:
        size = 128 * len(line)
        term = dot(jnp.concatenate(line, axis=1), gram[start : start + size], 1, 0)
        value, start = term if value is None else value + term, start + size
    return value[:, :128] + core_swap(value[:, 128:])


def shards(momentum):
    core = lax.axis_index(CORE)
    own = momentum.T
    low, high = own[:, :128], own[:, 128:]
    keep = jnp.where(core == 0, low, high)
    give = core_swap(jnp.where(core == 0, high, low))
    halves = [jnp.where(core == 0, keep, give), jnp.where(core == 0, give, keep)]
    lines = [z_line(half) for half in halves]
    pairs = []
    for half in halves:
        partner = y_swap(after(half, *lines[0][3:5], *lines[1][3:5]))
        pairs.append(jnp.concatenate([half, core_swap(half), partner, core_swap(partner)], axis=1))
    blocks = [dot(a, pairs[0], 0, 0) + dot(b, pairs[1], 0, 0) for a, b in zip(*lines)]
    blocks = jnp.stack(blocks).reshape(8, 4, 2, 16, 512)

    part, rest = sum_x(blocks[..., 256:]), sum_y_hi(blocks[..., :256])
    part, rest = lax.optimization_barrier((part, rest))
    part, rest = sum_y_hi(part) / COLS, sum_x(rest) / COLS
    part, rest = lax.optimization_barrier((part, rest))
    part, rest = spread_y_hi(part), spread_x(rest)
    part, rest = lax.optimization_barrier((part, rest))
    to_partner = spread_x(part).reshape(1024, 256)
    to_row = spread_y_hi(rest).reshape(1024, 256)

    crossed = [y_swap(share([line], to_partner)) for line in lines]
    inner = [
        weight_cub * half + weight_quint * (share([line], to_row) + value)
        for half, line, value in zip(halves, lines, crossed)
    ]
    lines = [z_line(value) for value in inner]
    lines = [(line[:5], line[5:]) for line in lines]
    crossed = [y_swap(share(line, to_partner)) for line in lines]
    outer = [weight_lin * half + (share(line, to_row) + value) for half, line, value in zip(halves, lines, crossed)]
    keep = jnp.where(core == 0, outer[0], outer[1])
    give = core_swap(jnp.where(core == 0, outer[1], outer[0]))
    return jnp.concatenate([jnp.where(core == 0, keep, give), jnp.where(core == 0, give, keep)], axis=1).T


def solution(mesh):
    parts = Mesh(mesh.devices.reshape(SIZES), (Y_LO, Z, X, Y_HI, CORE))
    spec = P((Y_LO, Z), (X, Y_HI, CORE))
    return jax.shard_map(shards, mesh=parts, in_specs=(spec,), out_specs=spec, check_vma=False)
```

```python
import jax
import jax.numpy as jnp
from jax import lax
from jax.experimental import pallas as pl
from jax.experimental.pallas import tpu as pltpu
from jax.sharding import Mesh
from jax.sharding import PartitionSpec as P

COLS = 7168

weight_lin = 3.4445
weight_cub = -4.775
weight_quint = 2.0315

Y_LO, Z, X, Y_HI, CORE = "y_lo", "z", "x", "y_hi", "core"
SIZES = (2, 8, 4, 2, 2)


def z_shift(value, step):
    return lax.ppermute(value, Z, [(i, (i + step) % 8) for i in range(8)])


def y_swap(value):
    return lax.ppermute(value, Y_LO, [(0, 1), (1, 0)])


def core_swap(value):
    return lax.ppermute(value, CORE, [(0, 1), (1, 0)])


def y_hi_swap(value):
    return lax.ppermute(value, Y_HI, [(0, 1), (1, 0)])


def x_shift(value, step):
    return lax.ppermute(value, X, [(i, (i + step) % 4) for i in range(4)])


def z_line(own):
    middle = own.shape[0] // 2
    p1, m1 = z_shift(own, -1), z_shift(own, 1)
    p2, m2 = z_shift(p1, -1), z_shift(m1, 1)
    p3, m3 = z_shift(p2, -1), z_shift(m2, 1)
    far = jnp.concatenate([z_shift(p3[:middle], -1), z_shift(m3[middle:], 1)], axis=0)
    return own, p1, m1, p2, m2, p3, m3, far


def split(value):
    high = value.astype(jnp.bfloat16)
    return high, (value - high.astype(jnp.float32)).astype(jnp.bfloat16)


def dot_split(left, right, dims):
    total = None
    for a, b in ((0, 0), (0, 1), (1, 0)):
        term = lax.dot_general(left[a], right[b], (dims, ((), ())), preferred_element_type=jnp.float32)
        total = term if total is None else total + term
    return total


def call(kernel, shapes, operands):
    return pl.pallas_call(
        kernel,
        out_shape=[jax.ShapeDtypeStruct(shape, jnp.float32) for shape in shapes],
        in_specs=[pl.BlockSpec(memory_space=pltpu.VMEM)] * len(operands),
        out_specs=[pl.BlockSpec(memory_space=pltpu.VMEM)] * len(shapes),
        compiler_params=pltpu.CompilerParams(vmem_limit_bytes=40 * 2**20),
        cost_estimate=pl.CostEstimate(flops=20 * 10**9, bytes_accessed=40 * 2**20, transcendentals=0),
    )(*operands)


def gram_kernel(*refs):
    total = None
    for part in range(2):
        here = refs[part * 12 : part * 12 + 12]
        line, (half, rest, partner, other) = here[:8], here[8:]
        turned = jnp.concatenate([other[224:, :], other[:224, :]], axis=0)
        left = split(jnp.concatenate([block[...] for block in line], axis=1))
        right = split(jnp.concatenate([half[...], rest[...], partner[...], turned], axis=1))
        term = dot_split(left, right, ((0,), (0,)))
        total = term if total is None else total + term
    refs[-2][...] = total[:, 256:]
    refs[-1][...] = total[:, :256]


def gram_blocks(lines, pairs):
    return call(gram_kernel, [(1024, 256)] * 2, [*lines[0], *pairs[0], *lines[1], *pairs[1]])


def product(line, gram, start=0, before=None):
    count = len(line)

    def kernel(*refs):
        left = split(jnp.concatenate([block[...] for block in refs[:count]], axis=1))
        right = split(refs[count][pl.ds(start * 128, count * 128), :])
        value = dot_split(left, right, ((1,), (0,)))
        refs[-1][...] = value if before is None else value + refs[count + 1][...]

    operands = [*line, gram] + ([] if before is None else [before])
    return call(kernel, [(448, 256)], operands)[0]


def sum_x(value):
    x = lax.axis_index(X)
    total = None
    for step in (2, 1, 3, 0):
        chunk = lax.dynamic_index_in_dim(value, (x + step) % 4, 1, keepdims=False)
        if step:
            chunk = x_shift(chunk, step)
        total = chunk if total is None else total + chunk
    return total


def sum_y_hi(value):
    low, high = value[..., 0, :, :], value[..., 1, :, :]
    first = lax.axis_index(Y_HI) == 0
    return jnp.where(first, low, high) + y_hi_swap(jnp.where(first, high, low))


def spread_y_hi(value):
    other = y_hi_swap(value)
    first = lax.axis_index(Y_HI) == 0
    return jnp.stack([jnp.where(first, value, other), jnp.where(first, other, value)], axis=-3)


def rotate(items, index):
    n = len(items)
    shift = 1
    while shift < n:
        bit = (index // shift) % 2 == 1
        items = [jnp.where(bit, items[(k - shift) % n], items[k]) for k in range(n)]
        shift *= 2
    return items


def spread_x(value):
    items = [value, x_shift(value, 3), x_shift(value, 2), x_shift(value, 1)]
    return jnp.stack(rotate(items, lax.axis_index(X)), axis=1)


def sum_cores(value):
    other = core_swap(value[:, 128:])
    return value[:, :128] + jnp.concatenate([other[224:], other[:224]], axis=0)


def together(*values):
    return lax.optimization_barrier(values)


def shards(momentum):
    core = lax.axis_index(CORE)
    own = momentum.T
    half = jnp.where(core == 0, own[:, :128], own[:, 128:])
    rest = jnp.where(core == 0, own[:, 128:], own[:, :128])
    got, got_rest = core_swap(rest), core_swap(half)
    halves, pairs = [], []
    for rows in (slice(0, 224), slice(224, 448)):
        value = jnp.concatenate([half[rows], got[rows]], axis=0)
        halves.append(value)
        partner = y_swap(value)
        pairs.append((value, jnp.concatenate([rest[rows], got_rest[rows]], axis=0), partner, core_swap(partner)))
    lines = [z_line(value) for value in halves]

    part, rest = gram_blocks(lines, pairs)
    part, rest = together(sum_x(part.reshape(8, 4, 2, 16, 256)), sum_y_hi(rest.reshape(8, 4, 2, 16, 256)))
    part, rest = together(sum_y_hi(part) / COLS, sum_x(rest) / COLS)
    part, rest = together(spread_y_hi(part), spread_x(rest))
    to_partner, to_row = spread_x(part).reshape(1024, 256), spread_y_hi(rest).reshape(1024, 256)

    crossed = [y_swap(sum_cores(product(line, to_partner))) for line in lines]
    direct = [sum_cores(product(line, to_row)) for line in lines]
    lines = [z_line(weight_cub * a + weight_quint * (b + c)) for a, b, c in zip(halves, direct, crossed)]
    outer = []
    for line in lines:
        crossed = product(line[5:], to_partner, 5, product(line[:5], to_partner))
        direct = product(line[5:], to_row, 5, product(line[:5], to_row))
        value = y_swap(sum_cores(crossed)) + sum_cores(direct)
        outer.append(jnp.concatenate([value[:224], core_swap(value[224:])], axis=1))
    value = jnp.concatenate(outer, axis=0)
    value = jnp.where(core == 0, value, jnp.concatenate([value[:, 128:], value[:, :128]], axis=1))
    return (weight_lin * own + value).T


def solution(mesh):
    parts = Mesh(mesh.devices.reshape(SIZES), (Y_LO, Z, X, Y_HI, CORE))
    spec = P((Y_LO, Z), (X, Y_HI, CORE))
    return jax.shard_map(shards, mesh=parts, in_specs=(spec,), out_specs=spec, check_vma=False)
```

```python
import functools

import jax
import jax.numpy as jnp
from jax import lax
from jax.experimental import pallas as pl
from jax.experimental.pallas import tpu as pltpu
from jax.sharding import Mesh
from jax.sharding import PartitionSpec as P

COLS = 7168

weight_lin = 3.4445
weight_cub = -4.775
weight_quint = 2.0315

Y_LO, Z, X, Y_HI, CORE = "y_lo", "z", "x", "y_hi", "core"
SIZES = (2, 8, 4, 2, 2)


def z_shift(value, step):
    return lax.ppermute(value, Z, [(i, (i + step) % 8) for i in range(8)])


def y_swap(value):
    return lax.ppermute(value, Y_LO, [(0, 1), (1, 0)])


def core_swap(value):
    return lax.ppermute(value, CORE, [(0, 1), (1, 0)])


def y_hi_swap(value):
    return lax.ppermute(value, Y_HI, [(0, 1), (1, 0)])


def x_shift(value, step):
    return lax.ppermute(value, X, [(i, (i + step) % 4) for i in range(4)])


def z_line(own, forward):
    p1, m1 = z_shift(own, -1), z_shift(own, 1)
    p2, m2 = z_shift(p1, -1), z_shift(m1, 1)
    p3, m3 = z_shift(p2, -1), z_shift(m2, 1)
    return own, p1, m1, p2, m2, p3, m3, z_shift(p3, -1) if forward else z_shift(m3, 1)


def split(value):
    high = value.astype(jnp.bfloat16)
    return high, (value - high.astype(jnp.float32)).astype(jnp.bfloat16)


def dot_split(left, right, dims):
    total = None
    for a, b in ((0, 0), (0, 1), (1, 0)):
        term = lax.dot_general(left[a], right[b], (dims, ((), ())), preferred_element_type=jnp.float32)
        total = term if total is None else total + term
    return total


def call(kernel, shapes, operands):
    return pl.pallas_call(
        kernel,
        out_shape=[jax.ShapeDtypeStruct(shape, jnp.float32) for shape in shapes],
        in_specs=[pl.BlockSpec(memory_space=pltpu.VMEM)] * len(operands),
        out_specs=[pl.BlockSpec(memory_space=pltpu.VMEM)] * len(shapes),
        compiler_params=pltpu.CompilerParams(vmem_limit_bytes=20 * 2**20),
        cost_estimate=pl.CostEstimate(flops=20 * 10**9, bytes_accessed=40 * 2**20, transcendentals=0),
    )(*operands)


def gram_kernel(line_count, turn, *refs):
    total = None
    for part in range(2):
        here = refs[part * (line_count + 2) : (part + 1) * (line_count + 2)]
        line, (first, second) = here[:line_count], here[line_count:]
        second = second[...]
        if turn:
            second = jnp.concatenate([second[224:], second[:224]], axis=0)
        left = split(jnp.concatenate([block[...] for block in line], axis=1))
        right = split(jnp.concatenate([first[...], second], axis=1))
        term = dot_split(left, right, ((0,), (0,)))
        total = term if total is None else total + term
    refs[-1][...] = total


def gram_blocks(lines, pairs, turn):
    operands = [*lines[0], *pairs[0], *lines[1], *pairs[1]]
    value = call(functools.partial(gram_kernel, 8, turn), [(1024, 256)], operands)[0]
    return value.reshape(8, 4, 2, 16, 256)


def product(line, gram, start=0, before=None):
    count = len(line)

    def kernel(*refs):
        left = split(jnp.concatenate([block[...] for block in refs[:count]], axis=1))
        right = split(refs[count][pl.ds(start * 128, count * 128), :])
        value = dot_split(left, right, ((1,), (0,)))
        refs[-1][...] = value if before is None else value + refs[count + 1][...]

    operands = [*line, gram] + ([] if before is None else [before])
    return call(kernel, [(448, 256)], operands)[0]


def sum_x(value):
    x = lax.axis_index(X)
    total = None
    for step in (2, 1, 3, 0):
        chunk = lax.dynamic_index_in_dim(value, (x + step) % 4, 1, keepdims=False)
        if step:
            chunk = x_shift(chunk, step)
        total = chunk if total is None else total + chunk
    return total


def sum_y_hi(value):
    low, high = value[..., 0, :, :], value[..., 1, :, :]
    first = lax.axis_index(Y_HI) == 0
    return jnp.where(first, low, high) + y_hi_swap(jnp.where(first, high, low))


def spread_y_hi(value):
    other = y_hi_swap(value)
    first = lax.axis_index(Y_HI) == 0
    return jnp.stack([jnp.where(first, value, other), jnp.where(first, other, value)], axis=-3)


def rotate(items, index):
    n = len(items)
    shift = 1
    while shift < n:
        bit = (index // shift) % 2 == 1
        items = [jnp.where(bit, items[(k - shift) % n], items[k]) for k in range(n)]
        shift *= 2
    return items


def spread_x(value):
    items = [value, x_shift(value, 3), x_shift(value, 2), x_shift(value, 1)]
    return jnp.stack(rotate(items, lax.axis_index(X)), axis=1)


def sum_cores(value):
    other = core_swap(value[:, 128:])
    return value[:, :128] + jnp.concatenate([other[224:], other[:224]], axis=0)


def sum_columns(value):
    other = core_swap(value[224:])
    return value[:224] + jnp.concatenate([other[:, 128:], other[:, :128]], axis=1)


def together(*values):
    return lax.optimization_barrier(values)


def shards(momentum):
    core = lax.axis_index(CORE)
    own = momentum.T
    half = jnp.where(core == 0, own[:, :128], own[:, 128:])
    rest = jnp.where(core == 0, own[:, 128:], own[:, :128])
    got, got_rest = core_swap(rest), core_swap(half)
    halves, pairs = [], []
    for rows in (slice(0, 224), slice(224, 448)):
        value = jnp.concatenate([half[rows], got[rows]], axis=0)
        halves.append(value)
        partner = y_swap(value)
        pairs.append((value, jnp.concatenate([rest[rows], got_rest[rows]], axis=0), partner, core_swap(partner)))
    lines = [z_line(value, part == 0) for part, value in enumerate(halves)]

    part = sum_x(gram_blocks(lines, [pair[2:] for pair in pairs], True))
    rest = sum_y_hi(gram_blocks(lines, [pair[:2] for pair in pairs], False))
    part, rest = together(part, rest)
    part, rest = together(sum_y_hi(part) / COLS, sum_x(rest) / COLS)
    part, rest = spread_y_hi(part), spread_x(rest)
    to_partner, to_row = spread_x(part).reshape(1024, 256), spread_y_hi(rest).reshape(1024, 256)

    crossed = [y_swap(sum_cores(product(line, to_partner))) for line in lines]
    direct = [sum_cores(product(line, to_row)) for line in lines]
    inner = [weight_cub * a + weight_quint * (b + c) for a, b, c in zip(halves, direct, crossed)]
    lines = [z_line(value, part == 0) for part, value in enumerate(inner)]
    outer = []
    for line in lines:
        crossed = sum_columns(product(line[5:], to_partner, 5, product(line[:5], to_partner)))
        direct = sum_columns(product(line[5:], to_row, 5, product(line[:5], to_row)))
        outer.append(y_swap(crossed) + direct)
    value = jnp.concatenate(outer, axis=0)
    value = jnp.where(core == 0, value, jnp.concatenate([value[:, 128:], value[:, :128]], axis=1))
    return (weight_lin * own + value).T


def solution(mesh):
    parts = Mesh(mesh.devices.reshape(SIZES), (Y_LO, Z, X, Y_HI, CORE))
    spec = P((Y_LO, Z), (X, Y_HI, CORE))
    return jax.shard_map(shards, mesh=parts, in_specs=(spec,), out_specs=spec, check_vma=False)
```

```python
import functools

import jax
import jax.numpy as jnp
from jax import lax
from jax.experimental import pallas as pl
from jax.experimental.pallas import tpu as pltpu
from jax.sharding import Mesh
from jax.sharding import PartitionSpec as P

COLS = 7168

weight_lin = 3.4445
weight_cub = -4.775
weight_quint = 2.0315

Y_LO, Z, X, Y_HI, CORE = "y_lo", "z", "x", "y_hi", "core"
SIZES = (2, 8, 4, 2, 2)


def z_shift(value, step):
    return lax.ppermute(value, Z, [(i, (i + step) % 8) for i in range(8)])


def y_swap(value):
    return lax.ppermute(value, Y_LO, [(0, 1), (1, 0)])


def core_swap(value):
    return lax.ppermute(value, CORE, [(0, 1), (1, 0)])


def y_hi_swap(value):
    return lax.ppermute(value, Y_HI, [(0, 1), (1, 0)])


def x_shift(value, step):
    return lax.ppermute(value, X, [(i, (i + step) % 4) for i in range(4)])


def z_line(own, forward):
    p1, m1 = z_shift(own, -1), z_shift(own, 1)
    p2, m2 = z_shift(p1, -1), z_shift(m1, 1)
    p3, m3 = z_shift(p2, -1), z_shift(m2, 1)
    return own, p1, m1, p2, m2, p3, m3, z_shift(p3, -1) if forward else z_shift(m3, 1)


def split(value):
    high = value.astype(jnp.bfloat16)
    return high, (value - high.astype(jnp.float32)).astype(jnp.bfloat16)


def dot_split(left, right, dims):
    total = None
    for a, b in ((0, 0), (0, 1), (1, 0)):
        term = lax.dot_general(left[a], right[b], (dims, ((), ())), preferred_element_type=jnp.float32)
        total = term if total is None else total + term
    return total


def call(kernel, shapes, operands):
    return pl.pallas_call(
        kernel,
        out_shape=[jax.ShapeDtypeStruct(shape, jnp.float32) for shape in shapes],
        in_specs=[pl.BlockSpec(memory_space=pltpu.VMEM)] * len(operands),
        out_specs=[pl.BlockSpec(memory_space=pltpu.VMEM)] * len(shapes),
        compiler_params=pltpu.CompilerParams(vmem_limit_bytes=20 * 2**20),
        cost_estimate=pl.CostEstimate(flops=20 * 10**9, bytes_accessed=40 * 2**20, transcendentals=0),
    )(*operands)


def gram_kernel(line_count, turn, *refs):
    total = None
    for part in range(2):
        here = refs[part * (line_count + 2) : (part + 1) * (line_count + 2)]
        line, (first, second) = here[:line_count], here[line_count:]
        second = second[...]
        if turn:
            second = jnp.concatenate([second[224:], second[:224]], axis=0)
        left = split(jnp.concatenate([block[...] for block in line], axis=1))
        right = split(jnp.concatenate([first[...], second], axis=1))
        term = dot_split(left, right, ((0,), (0,)))
        total = term if total is None else total + term
    refs[-1][...] = total


def gram_blocks(lines, pairs, turn):
    operands = [*lines[0], *pairs[0], *lines[1], *pairs[1]]
    count = len(lines[0])
    value = call(functools.partial(gram_kernel, count, turn), [(count * 128, 256)], operands)[0]
    return value.reshape(count, 4, 2, 16, 256)


def product(line, gram, start=0, before=None):
    count = len(line)

    def kernel(*refs):
        left = split(jnp.concatenate([block[...] for block in refs[:count]], axis=1))
        right = split(refs[count][pl.ds(start * 128, count * 128), :])
        value = dot_split(left, right, ((1,), (0,)))
        refs[-1][...] = value if before is None else value + refs[count + 1][...]

    operands = [*line, gram] + ([] if before is None else [before])
    return call(kernel, [(448, 256)], operands)[0]


def sum_x(value):
    x = lax.axis_index(X)
    total = None
    for step in (3, 2, 1, 0):
        chunk = lax.dynamic_index_in_dim(value, (x + step) % 4, 1, keepdims=False)
        if step:
            chunk = x_shift(chunk, step)
        total = chunk if total is None else total + chunk
    return total


def sum_y_hi(value):
    low, high = value[..., 0, :, :], value[..., 1, :, :]
    first = lax.axis_index(Y_HI) == 0
    return jnp.where(first, low, high) + y_hi_swap(jnp.where(first, high, low))


def spread_y_hi(value):
    other = y_hi_swap(value)
    first = lax.axis_index(Y_HI) == 0
    return jnp.stack([jnp.where(first, value, other), jnp.where(first, other, value)], axis=-3)


def rotate(items, index):
    n = len(items)
    shift = 1
    while shift < n:
        bit = (index // shift) % 2 == 1
        items = [jnp.where(bit, items[(k - shift) % n], items[k]) for k in range(n)]
        shift *= 2
    return items


def spread_x(value):
    items = [value, x_shift(value, 3), x_shift(value, 2), x_shift(value, 1)]
    return jnp.stack(rotate(items, lax.axis_index(X)), axis=1)


def sum_cores(value):
    other = core_swap(value[:, 128:])
    return value[:, :128] + jnp.concatenate([other[224:], other[:224]], axis=0)


def sum_columns(value):
    other = core_swap(value[224:])
    return value[:224] + jnp.concatenate([other[:, 128:], other[:, :128]], axis=1)


def together(*values):
    return lax.optimization_barrier(values)


def shards(momentum):
    core = lax.axis_index(CORE)
    own = momentum.T
    half = jnp.where(core == 0, own[:, :128], own[:, 128:])
    rest = jnp.where(core == 0, own[:, 128:], own[:, :128])
    got, got_rest = core_swap(rest), core_swap(half)
    halves, pairs = [], []
    for rows in (slice(0, 224), slice(224, 448)):
        value = jnp.concatenate([half[rows], got[rows]], axis=0)
        halves.append(value)
        partner = y_swap(value)
        pairs.append((value, jnp.concatenate([rest[rows], got_rest[rows]], axis=0), partner, core_swap(partner)))
    lines = [z_line(value, part == 0) for part, value in enumerate(halves)]

    part = sum_x(gram_blocks(lines, [pair[2:] for pair in pairs], True))
    rest = sum_y_hi(jnp.concatenate([gram_blocks([line[part] for line in lines], [pair[:2] for pair in pairs], False) for part in (slice(0, 5), slice(5, 8))]))
    part, rest = together(part, rest)
    part, rest = together(sum_y_hi(part) / COLS, sum_x(rest) / COLS)
    part, rest = spread_y_hi(part), spread_x(rest)
    to_partner, to_row = spread_x(part).reshape(1024, 256), spread_y_hi(rest).reshape(1024, 256)

    crossed = [y_swap(sum_cores(product(line, to_partner))) for line in lines]
    direct = [sum_cores(product(line, to_row)) for line in lines]
    inner = [weight_cub * a + weight_quint * (b + c) for a, b, c in zip(halves, direct, crossed)]
    lines = [z_line(value, part == 0) for part, value in enumerate(inner)]
    outer = []
    for line in lines:
        crossed = sum_columns(product(line[5:], to_partner, 5, product(line[:5], to_partner)))
        direct = sum_columns(product(line[5:], to_row, 5, product(line[:5], to_row)))
        outer.append(y_swap(crossed) + direct)
    value = jnp.concatenate(outer, axis=0)
    value = jnp.where(core == 0, value, jnp.concatenate([value[:, 128:], value[:, :128]], axis=1))
    return (weight_lin * own + value).T


def solution(mesh):
    parts = Mesh(mesh.devices.reshape(SIZES), (Y_LO, Z, X, Y_HI, CORE))
    spec = P((Y_LO, Z), (X, Y_HI, CORE))
    return jax.shard_map(shards, mesh=parts, in_specs=(spec,), out_specs=spec, check_vma=False)
```

```python
import functools

import jax
import jax.numpy as jnp
from jax import lax
from jax.experimental import pallas as pl
from jax.experimental.pallas import tpu as pltpu
from jax.sharding import Mesh
from jax.sharding import PartitionSpec as P

COLS = 7168

weight_lin = 3.4445
weight_cub = -4.775
weight_quint = 2.0315

Y_LO, Z, X, Y_HI, CORE = "y_lo", "z", "x", "y_hi", "core"
SIZES = (2, 8, 4, 2, 2)


def z_shift(value, step):
    return lax.ppermute(value, Z, [(i, (i + step) % 8) for i in range(8)])


def y_swap(value):
    return lax.ppermute(value, Y_LO, [(0, 1), (1, 0)])


def core_swap(value):
    return lax.ppermute(value, CORE, [(0, 1), (1, 0)])


def y_hi_swap(value):
    return lax.ppermute(value, Y_HI, [(0, 1), (1, 0)])


def x_shift(value, step):
    return lax.ppermute(value, X, [(i, (i + step) % 4) for i in range(4)])


def z_line(own, forward):
    p1, m1 = z_shift(own, -1), z_shift(own, 1)
    p2, m2 = z_shift(p1, -1), z_shift(m1, 1)
    p3, m3 = z_shift(p2, -1), z_shift(m2, 1)
    return own, p1, m1, p2, m2, p3, m3, z_shift(p3, -1) if forward else z_shift(m3, 1)


def split(value):
    high = value.astype(jnp.bfloat16)
    return high, (value - high.astype(jnp.float32)).astype(jnp.bfloat16)


def dot_split(left, right, dims):
    total = None
    for a, b in ((0, 0), (0, 1), (1, 0)):
        term = lax.dot_general(left[a], right[b], (dims, ((), ())), preferred_element_type=jnp.float32)
        total = term if total is None else total + term
    return total


def call(kernel, shapes, operands):
    return pl.pallas_call(
        kernel,
        out_shape=[jax.ShapeDtypeStruct(shape, jnp.float32) for shape in shapes],
        in_specs=[pl.BlockSpec(memory_space=pltpu.VMEM)] * len(operands),
        out_specs=[pl.BlockSpec(memory_space=pltpu.VMEM)] * len(shapes),
        compiler_params=pltpu.CompilerParams(vmem_limit_bytes=20 * 2**20),
        cost_estimate=pl.CostEstimate(flops=20 * 10**9, bytes_accessed=40 * 2**20, transcendentals=0),
    )(*operands)


def gram_kernel(line_count, turn, *refs):
    total = None
    for part in range(2):
        here = refs[part * (line_count + 2) : (part + 1) * (line_count + 2)]
        line, (first, second) = here[:line_count], here[line_count:]
        second = second[...]
        if turn:
            second = jnp.concatenate([second[224:], second[:224]], axis=0)
        left = split(jnp.concatenate([block[...] for block in line], axis=1))
        right = split(jnp.concatenate([first[...], second], axis=1))
        term = dot_split(left, right, ((0,), (0,)))
        total = term if total is None else total + term
    refs[-1][...] = total


def gram_blocks(lines, pairs, turn):
    operands = [*lines[0], *pairs[0], *lines[1], *pairs[1]]
    count = len(lines[0])
    value = call(functools.partial(gram_kernel, count, turn), [(count * 128, 256)], operands)[0]
    return value.reshape(count, 4, 2, 16, 256)


def product(line, gram, start=0, before=None):
    count = len(line)

    def kernel(*refs):
        left = split(jnp.concatenate([block[...] for block in refs[:count]], axis=1))
        right = split(refs[count][pl.ds(start * 128, count * 128), :])
        value = dot_split(left, right, ((1,), (0,)))
        refs[-1][...] = value if before is None else value + refs[count + 1][...]

    operands = [*line, gram] + ([] if before is None else [before])
    return call(kernel, [(448, 256)], operands)[0]


def sum_x(value):
    x = lax.axis_index(X)
    total = None
    for step in (3, 2, 1, 0):
        chunk = lax.dynamic_index_in_dim(value, (x + step) % 4, 1, keepdims=False)
        if step:
            chunk = x_shift(chunk, step)
        total = chunk if total is None else total + chunk
    return total


def sum_y_hi(value):
    low, high = value[..., 0, :, :], value[..., 1, :, :]
    first = lax.axis_index(Y_HI) == 0
    return jnp.where(first, low, high) + y_hi_swap(jnp.where(first, high, low))


def spread_y_hi(value):
    other = y_hi_swap(value)
    first = lax.axis_index(Y_HI) == 0
    return jnp.stack([jnp.where(first, value, other), jnp.where(first, other, value)], axis=-3)


def rotate(items, index):
    n = len(items)
    shift = 1
    while shift < n:
        bit = (index // shift) % 2 == 1
        items = [jnp.where(bit, items[(k - shift) % n], items[k]) for k in range(n)]
        shift *= 2
    return items


def spread_x(value):
    items = [value, x_shift(value, 3), x_shift(value, 2), x_shift(value, 1)]
    return jnp.stack(rotate(items, lax.axis_index(X)), axis=1)


def sum_cores(value):
    other = core_swap(value[:, 128:])
    return value[:, :128] + jnp.concatenate([other[224:], other[:224]], axis=0)


def sum_columns(value):
    other = core_swap(value[224:])
    return value[:224] + jnp.concatenate([other[:, 128:], other[:, :128]], axis=1)


def together(*values):
    return lax.optimization_barrier(values)


def shards(momentum):
    core = lax.axis_index(CORE)
    own = momentum.T
    half = jnp.where(core == 0, own[:, :128], own[:, 128:])
    rest = jnp.where(core == 0, own[:, 128:], own[:, :128])
    got, got_rest = core_swap(rest), core_swap(half)
    halves, pairs = [], []
    for rows in (slice(0, 224), slice(224, 448)):
        value = jnp.concatenate([half[rows], got[rows]], axis=0)
        halves.append(value)
        partner = y_swap(value)
        pairs.append((value, jnp.concatenate([rest[rows], got_rest[rows]], axis=0), partner, core_swap(partner)))
    lines = [z_line(value, part == 0) for part, value in enumerate(halves)]

    part = sum_x(gram_blocks(lines, [pair[2:] for pair in pairs], True))
    rest = sum_y_hi(jnp.concatenate([gram_blocks([line[part] for line in lines], [pair[:2] for pair in pairs], False) for part in (slice(0, 5), slice(5, 8))]))
    part, rest = together(part, rest)
    part, rest = sum_y_hi(part) / COLS, sum_x(rest) / COLS
    part, rest = spread_y_hi(part), spread_x(rest)
    to_partner, to_row = spread_x(part).reshape(1024, 256), spread_y_hi(rest).reshape(1024, 256)

    crossed = [y_swap(sum_cores(product(line, to_partner))) for line in lines]
    direct = [sum_cores(product(line, to_row)) for line in lines]
    inner = [weight_cub * a + weight_quint * (b + c) for a, b, c in zip(halves, direct, crossed)]
    lines = [z_line(value, part == 0) for part, value in enumerate(inner)]
    outer = []
    for line in lines:
        crossed = sum_columns(product(line[5:], to_partner, 5, product(line[:5], to_partner)))
        direct = sum_columns(product(line[5:], to_row, 5, product(line[:5], to_row)))
        outer.append(y_swap(crossed) + direct)
    value = jnp.concatenate(outer, axis=0)
    value = jnp.where(core == 0, value, jnp.concatenate([value[:, 128:], value[:, :128]], axis=1))
    return (weight_lin * own + value).T


def solution(mesh):
    parts = Mesh(mesh.devices.reshape(SIZES), (Y_LO, Z, X, Y_HI, CORE))
    spec = P((Y_LO, Z), (X, Y_HI, CORE))
    return jax.shard_map(shards, mesh=parts, in_specs=(spec,), out_specs=spec, check_vma=False)
```

```python
import functools

import jax
import jax.numpy as jnp
from jax import lax
from jax.experimental import pallas as pl
from jax.experimental.pallas import tpu as pltpu
from jax.sharding import Mesh
from jax.sharding import PartitionSpec as P

COLS = 7168

weight_lin = 3.4445
weight_cub = -4.775
weight_quint = 2.0315

Y_LO, Z, X, Y_HI, CORE = "y_lo", "z", "x", "y_hi", "core"
SIZES = (2, 8, 4, 2, 2)


def z_shift(value, step):
    return lax.ppermute(value, Z, [(i, (i + step) % 8) for i in range(8)])


def y_swap(value):
    return lax.ppermute(value, Y_LO, [(0, 1), (1, 0)])


def core_swap(value):
    return lax.ppermute(value, CORE, [(0, 1), (1, 0)])


def y_hi_swap(value):
    return lax.ppermute(value, Y_HI, [(0, 1), (1, 0)])


def x_shift(value, step):
    return lax.ppermute(value, X, [(i, (i + step) % 4) for i in range(4)])


def z_line(own, forward):
    p1, m1 = z_shift(own, -1), z_shift(own, 1)
    p2, m2 = z_shift(p1, -1), z_shift(m1, 1)
    p3, m3 = z_shift(p2, -1), z_shift(m2, 1)
    return own, p1, m1, p2, m2, p3, m3, z_shift(p3, -1) if forward else z_shift(m3, 1)


def split(value):
    high = value.astype(jnp.bfloat16)
    return high, (value - high.astype(jnp.float32)).astype(jnp.bfloat16)


def dot_split(left, right, dims):
    total = None
    for a, b in ((0, 0), (0, 1), (1, 0)):
        term = lax.dot_general(left[a], right[b], (dims, ((), ())), preferred_element_type=jnp.float32)
        total = term if total is None else total + term
    return total


def call(kernel, shapes, operands):
    return pl.pallas_call(
        kernel,
        out_shape=[jax.ShapeDtypeStruct(shape, jnp.float32) for shape in shapes],
        in_specs=[pl.BlockSpec(memory_space=pltpu.VMEM)] * len(operands),
        out_specs=[pl.BlockSpec(memory_space=pltpu.VMEM)] * len(shapes),
        compiler_params=pltpu.CompilerParams(vmem_limit_bytes=20 * 2**20),
        cost_estimate=pl.CostEstimate(flops=20 * 10**9, bytes_accessed=40 * 2**20, transcendentals=0),
    )(*operands)


def gram_kernel(line_count, turn, *refs):
    total = None
    for part in range(2):
        here = refs[part * (line_count + 2) : (part + 1) * (line_count + 2)]
        line, (first, second) = here[:line_count], here[line_count:]
        second = second[...]
        if turn:
            second = jnp.concatenate([second[224:], second[:224]], axis=0)
        left = split(jnp.concatenate([block[...] for block in line], axis=1))
        right = split(jnp.concatenate([first[...], second], axis=1))
        term = dot_split(left, right, ((0,), (0,)))
        total = term if total is None else total + term
    refs[-1][...] = total


def gram_blocks(lines, pairs, turn):
    operands = [*lines[0], *pairs[0], *lines[1], *pairs[1]]
    count = len(lines[0])
    value = call(functools.partial(gram_kernel, count, turn), [(count * 128, 256)], operands)[0]
    return value.reshape(count, 4, 2, 16, 256)


def product(line, gram, start=0, before=None):
    count = len(line)

    def kernel(*refs):
        left = split(jnp.concatenate([block[...] for block in refs[:count]], axis=1))
        right = split(refs[count][pl.ds(start * 128, count * 128), :])
        value = dot_split(left, right, ((1,), (0,)))
        refs[-1][...] = value if before is None else value + refs[count + 1][...]

    operands = [*line, gram] + ([] if before is None else [before])
    return call(kernel, [(448, 256)], operands)[0]


def far_product(lines, gram, before):
    count = len(lines[0]) - 5

    def kernel(*refs):
        right = split(refs[2 * count][pl.ds(640, count * 128), :])
        for part in range(2):
            line = refs[part * count : part * count + count]
            left = split(jnp.concatenate([block[...] for block in line], axis=1))
            value = dot_split(left, right, ((1,), (0,))) + refs[2 * count + 1 + part][...]
            refs[-2][pl.ds(224 * part, 224), :] = value[:224]
            refs[-1][pl.ds(224 * part, 224), :] = value[224:]

    return call(kernel, [(448, 256)] * 2, [*lines[0][5:], *lines[1][5:], gram, *before])


def sum_x(value):
    x = lax.axis_index(X)
    total = None
    for step in (3, 2, 1, 0):
        chunk = lax.dynamic_index_in_dim(value, (x + step) % 4, 1, keepdims=False)
        if step:
            chunk = x_shift(chunk, step)
        total = chunk if total is None else total + chunk
    return total


def sum_y_hi(value):
    low, high = value[..., 0, :, :], value[..., 1, :, :]
    first = lax.axis_index(Y_HI) == 0
    return jnp.where(first, low, high) + y_hi_swap(jnp.where(first, high, low))


def spread_y_hi(value):
    other = y_hi_swap(value)
    first = lax.axis_index(Y_HI) == 0
    return jnp.stack([jnp.where(first, value, other), jnp.where(first, other, value)], axis=-3)


def rotate(items, index):
    n = len(items)
    shift = 1
    while shift < n:
        bit = (index // shift) % 2 == 1
        items = [jnp.where(bit, items[(k - shift) % n], items[k]) for k in range(n)]
        shift *= 2
    return items


def spread_x(value):
    items = [value, x_shift(value, 3), x_shift(value, 2), x_shift(value, 1)]
    return jnp.stack(rotate(items, lax.axis_index(X)), axis=1)


def sum_cores(value):
    other = core_swap(value[:, 128:])
    return value[:, :128] + jnp.concatenate([other[224:], other[:224]], axis=0)


def sum_columns(mine, theirs):
    other = core_swap(theirs)
    return mine + jnp.concatenate([other[:, 128:], other[:, :128]], axis=1)


def together(*values):
    return lax.optimization_barrier(values)


def shards(momentum):
    core = lax.axis_index(CORE)
    own = momentum.T
    half = jnp.where(core == 0, own[:, :128], own[:, 128:])
    rest = jnp.where(core == 0, own[:, 128:], own[:, :128])
    got, got_rest = core_swap(rest), core_swap(half)
    halves, pairs = [], []
    for rows in (slice(0, 224), slice(224, 448)):
        value = jnp.concatenate([half[rows], got[rows]], axis=0)
        halves.append(value)
        partner = y_swap(value)
        pairs.append((value, jnp.concatenate([rest[rows], got_rest[rows]], axis=0), partner, core_swap(partner)))
    lines = [z_line(value, part == 1) for part, value in enumerate(halves)]

    part = sum_x(gram_blocks(lines, [pair[2:] for pair in pairs], True))
    rest = sum_y_hi(jnp.concatenate([gram_blocks([line[part] for line in lines], [pair[:2] for pair in pairs], False) for part in (slice(0, 5), slice(5, 8))]))
    part, rest = together(part, rest)
    part, rest = sum_y_hi(part) / COLS, sum_x(rest) / COLS
    part, rest = spread_y_hi(part), spread_x(rest)
    to_partner, to_row = spread_x(part).reshape(1024, 256), spread_y_hi(rest).reshape(1024, 256)

    crossed = [y_swap(sum_cores(product(line, to_partner))) for line in lines]
    direct = [sum_cores(product(line, to_row)) for line in lines]
    inner = [weight_cub * a + weight_quint * (b + c) for a, b, c in zip(halves, direct, crossed)]
    lines = [z_line(value, part == 1) for part, value in enumerate(inner)]
    early = [[product(line[:5], gram) for line in lines] for gram in (to_partner, to_row)]
    crossed = sum_columns(*far_product(lines, to_partner, early[0]))
    value = y_swap(crossed) + sum_columns(*far_product(lines, to_row, early[1]))
    value = jnp.where(core == 0, value, jnp.concatenate([value[:, 128:], value[:, :128]], axis=1))
    return (weight_lin * own + value).T


def solution(mesh):
    parts = Mesh(mesh.devices.reshape(SIZES), (Y_LO, Z, X, Y_HI, CORE))
    spec = P((Y_LO, Z), (X, Y_HI, CORE))
    return jax.shard_map(shards, mesh=parts, in_specs=(spec,), out_specs=spec, check_vma=False)
```
